32 devices in a mesh: groups: 2 (over y), seq: 4 (over z), blk: 4 (over x, core).
Axes of the slice: x: 2, y: 2, z: 4, core: 2. Of those that a mesh axis runs over, the one named last changes fastest.
Arguments:
- candidates: bfloat16 [8, 512, 512], P(('groups', 'blk'), 'seq'), parts along dimension 0, may hold values from -6 to 6
- gate_values: bfloat16 [8, 512, 512], P(('groups', 'blk'), 'seq'), parts along dimension 0, may hold values from -6 to 6
- hist_keys: bfloat16 [16384, 512], P(('groups', 'seq', 'blk')), parts along dimension 0, may hold values from -6 to 6
- hist_values: bfloat16 [16384, 512], P(('groups', 'seq', 'blk')), parts along dimension 0, may hold values from -17 to 17
- pattern: int32 [32, 16], P('groups'), parts along dimension 0, may hold values from 0 to 1, as said below
Outputs:
- result: bfloat16 [8, 512, 512], P(('groups', 'blk'), 'seq'), parts along dimension 0
The draws below stay inside these ranges and needn't reach their ends.
There are 2 independent parts, one for each index of `groups`. The reference program is written for one: setup_inputs(seed, part) draws one part's arguments, and reference() takes and returns one part's arrays. A program takes and returns all parts, laid end to end along the dimension named above; each array names one. Nothing has to cross between parts.
Inputs may be any that keep to these rules, and one draw needn't show every extreme that they name: `pattern`: every entry is 0 or 1; the last history block is admitted for every candidate block.
All inputs are finite; a program needn't handle non-finite values.
Results may differ from the reference program's by a relative error of at most 0.005.
Values may be sent and summed in bfloat16 or wider, within the bound.
No kernel may reach another device: no remote copies, remote signals or barrier semaphores. Data moves between devices by JAX's collectives and lax.ppermute only.
A program may use at most 64 MiB of HBM per device.

```python
import jax
import jax.numpy as jnp
from jax import lax

HEADS = 4
HEAD_DIM = 128
D = 512
CAND_BLOCK = 128
HIST_BLOCK = 512
CAND_SUB = 512
SUBGROUPS = 4
CANDS = 2048
CAND_BLOCKS = 16
HIST_BLOCKS = 16
HIST = 8192


def draw_hist_values(key, part):
    key = jax.random.fold_in(key, 11)
    noise_key, scale_key = jax.random.split(key)
    noise = jnp.clip(jax.random.normal(noise_key, (HIST, D), jnp.float32), -5.0, 5.0)
    scales = jnp.exp(jax.random.uniform(scale_key, (1, D), jnp.float32, 0.0, 2.3)) / 3.0
    return (noise * scales).astype(jnp.bfloat16)


def draw_pattern(key, part):
    key = jax.random.fold_in(key, 7)
    rolls = jax.random.randint(key, (CAND_BLOCKS, HIST_BLOCKS), 0, 1000)
    ramp = 100 + 800 * jnp.arange(HIST_BLOCKS, dtype=jnp.int32) // max(HIST_BLOCKS - 1, 1)
    admitted = (rolls < ramp[None, :]).astype(jnp.int32)
    return admitted.at[:, HIST_BLOCKS - 1].set(1)


def level_of(key, dims, pieces, smallest, largest):
    level = 1.0
    for axis_at, blocks in pieces:
        heights = jax.random.uniform(jax.random.fold_in(jax.random.fold_in(key, 6), axis_at), (blocks,), jnp.float32, smallest / len(pieces), largest / len(pieces))
        level = level * jnp.repeat(jnp.exp(heights), dims[axis_at] // blocks).reshape((-1,) + (1,) * (len(dims) - 1 - axis_at))
    return level


def normal_values(stream_key, extent, deviation, bound, cuts=(), kind=jnp.bfloat16):
    drawn = deviation * jax.random.normal(stream_key, extent, jnp.float32)
    if cuts:
        drawn = drawn * level_of(stream_key, extent, cuts, -0.22, 0.18)
    return jnp.clip(drawn, -bound, bound).astype(kind)


def setup_inputs(seed: int = 0, part: int = 0) -> dict:
    key_list = jax.random.split(jax.random.key(seed), 6)
    own_keys = jax.random.split(jax.random.fold_in(key_list[5], part), 6)
    return {
        "candidates": normal_values(own_keys[0], (SUBGROUPS, CAND_SUB, D), 1.0, 6.0, ((0, 4), (1, 4))),
        "gate_values": normal_values(own_keys[1], (SUBGROUPS, CAND_SUB, D), 1.0, 6.0, ((0, 4), (1, 4))),
        "hist_keys": normal_values(own_keys[2], (HIST, D), 1.0, 6.0, ((0, 16),)),
        "hist_values": draw_hist_values(jax.random.fold_in(jax.random.fold_in(key_list[5], part), 71), part),
        "pattern": draw_pattern(jax.random.fold_in(jax.random.fold_in(key_list[5], part), 71), part),
    }


def reference(candidates, gate_values, hist_keys, hist_values, pattern):
    queries = candidates.reshape(CANDS, D)
    query_heads = queries.reshape(CANDS, HEADS, HEAD_DIM).astype(jnp.float32)

    def absorb(running, block_index):
        key_block = lax.dynamic_slice_in_dim(hist_keys, block_index * HIST_BLOCK, HIST_BLOCK, 0)
        value_block = lax.dynamic_slice_in_dim(hist_values, block_index * HIST_BLOCK, HIST_BLOCK, 0)
        key_heads = key_block.reshape(HIST_BLOCK, HEADS, HEAD_DIM).astype(jnp.float32)
        value_heads = value_block.reshape(HIST_BLOCK, HEADS, HEAD_DIM).astype(jnp.float32)
        column = lax.dynamic_slice_in_dim(pattern, block_index, 1, 1)[:, 0]
        live_rows = jnp.repeat(column.astype(jnp.float32), CAND_BLOCK)
        scores = jnp.einsum('qhd,khd->hqk', query_heads, key_heads)
        weights = (jax.nn.silu(scores * HEAD_DIM ** (-0.5)) * live_rows[None, :, None]).astype(jnp.bfloat16)
        mixed = jnp.einsum('hqk,khd->qhd', weights.astype(jnp.float32), value_heads)
        return (running + mixed.reshape(CANDS, D), None)
    summed, ignored = lax.scan(absorb, jnp.zeros((CANDS, D), jnp.float32), jnp.arange(HIST_BLOCKS, dtype=jnp.int32))
    mean_square = lax.optimization_barrier(jnp.mean(summed * summed, axis=1, keepdims=True))
    normed = summed * lax.rsqrt(mean_square + 1e-05)
    gated = normed * gate_values.reshape(CANDS, D).astype(jnp.float32)
    return gated.astype(jnp.bfloat16).reshape(SUBGROUPS, CAND_SUB, D)
```

```python
import functools

import jax
import jax.numpy as jnp
from jax import lax
from jax.experimental import pallas as pl
from jax.experimental.pallas import tpu as pltpu
from jax.sharding import PartitionSpec as P

HEADS = 4
HEAD_DIM = 128
CAND_BLOCK = 128
HALF_SCALE = 0.5 * HEAD_DIM ** (-0.5)
CHUNKS = ((0, 1), (2, 3))
VMEM_LIMIT = 48 * 1024 * 1024


def swapped(block, axis, mask):
    size = lax.axis_size(axis)
    return lax.ppermute(block, axis, [(i, i ^ mask) for i in range(size)])


def attend_kernel(heads, row_count, block_masks, hist_masks, has_start, *refs):
    pattern_ref, refs = refs[0], refs[1:]
    row_refs, refs = refs[:row_count], refs[row_count:]
    hist_refs, refs = refs[: len(hist_masks)], refs[len(hist_masks) :]
    start_refs, refs = (refs[:row_count], refs[row_count:]) if has_start else (None, refs)
    out_refs = refs
    seq = lax.axis_index("seq")
    blk = lax.axis_index("blk")
    blk_size = lax.axis_size("blk")
    live = []
    for mask in hist_masks:
        column = seq * blk_size + (blk ^ mask)
        live.append(
            [
                pattern_ref[blk * row_count + place, column].astype(jnp.float32) * HALF_SCALE
                for place in [(seq ^ m) if m is not None else i for i, m in enumerate(block_masks)]
            ]
        )
    width = len(heads) * HEAD_DIM
    for at, head in enumerate(heads):
        queries = jnp.concatenate(
            [ref[:, head * HEAD_DIM : (head + 1) * HEAD_DIM] for ref in row_refs], axis=0
        )
        total = None
        for hist_ref, scales in zip(hist_refs, live):
            keys = hist_ref[:, at * HEAD_DIM : (at + 1) * HEAD_DIM]
            values = hist_ref[:, width + at * HEAD_DIM : width + (at + 1) * HEAD_DIM]
            scores = lax.dot_general(
                queries, keys, (((1,), (1,)), ((), ())), preferred_element_type=jnp.float32
            )
            weights = []
            for i, scale in enumerate(scales):
                half = scores[i * CAND_BLOCK : (i + 1) * CAND_BLOCK] * scale
                weights.append((half + half * jnp.tanh(half)).astype(jnp.bfloat16))
            mixed = jnp.dot(
                jnp.concatenate(weights, axis=0), values, preferred_element_type=jnp.float32
            )
            total = mixed if total is None else total + mixed
        for i, out_ref in enumerate(out_refs):
            piece = total[i * CAND_BLOCK : (i + 1) * CAND_BLOCK]
            columns = slice(at * HEAD_DIM, (at + 1) * HEAD_DIM)
            if has_start:
                piece = piece + start_refs[i][:, columns]
            out_ref[:, columns] = piece.astype(out_ref.dtype)


def attend(pattern, rows, hist, heads, block_masks, hist_masks, start=None, kinds=None):
    row_count = len(rows)
    width = len(heads) * HEAD_DIM
    kinds = kinds or [jnp.float32] * row_count
    events = hist[0].shape[0]
    flops = 4 * row_count * CAND_BLOCK * events * len(hist) * width
    inputs = [pattern, *rows, *hist, *(start or [])]
    vmem = pl.BlockSpec(memory_space=pltpu.VMEM)
    return pl.pallas_call(
        functools.partial(
            attend_kernel, heads, row_count, block_masks, hist_masks, start is not None
        ),
        out_shape=[jax.ShapeDtypeStruct((CAND_BLOCK, width), kind) for kind in kinds],
        in_specs=[pl.BlockSpec(memory_space=pltpu.SMEM)] + [vmem] * (len(inputs) - 1),
        out_specs=[vmem] * row_count,
        compiler_params=pltpu.CompilerParams(vmem_limit_bytes=VMEM_LIMIT),
        cost_estimate=pl.CostEstimate(
            flops=flops,
            transcendentals=flops // (4 * HEAD_DIM),
            bytes_accessed=sum(x.size * x.dtype.itemsize for x in inputs),
        ),
    )(*inputs)


def finish_kernel(parts, gate_ref, *refs):
    out_ref = refs[-1]
    summed, at = [], 0
    for count in parts:
        total = refs[at][...].astype(jnp.float32)
        for ref in refs[at + 1 : at + count]:
            total = total + ref[...].astype(jnp.float32)
        summed.append(total)
        at += count
    summed = jnp.concatenate(summed, axis=1)
    mean_square = jnp.mean(summed * summed, axis=1, keepdims=True)
    normed = summed * lax.rsqrt(mean_square + 1e-05)
    out_ref[...] = (normed * gate_ref[...].astype(jnp.float32)).astype(out_ref.dtype)


def finish(gate, pieces):
    arrays = [x for piece in pieces for x in piece]
    vmem = pl.BlockSpec(memory_space=pltpu.VMEM)
    return pl.pallas_call(
        functools.partial(finish_kernel, [len(piece) for piece in pieces]),
        out_shape=jax.ShapeDtypeStruct(gate.shape, gate.dtype),
        in_specs=[vmem] * (1 + len(arrays)),
        out_specs=vmem,
    )(gate, *arrays)


def gather_rows(block):
    if lax.axis_size("seq") == 4 and block.shape[0] == CAND_BLOCK:
        far = swapped(block, "seq", 2)
        near = swapped(block, "seq", 1)
        return [block, near, far, swapped(far, "seq", 1)], [0, 1, 2, 3]
    rows = lax.all_gather(block, "seq", axis=0, tiled=True)
    count = rows.shape[0] // CAND_BLOCK
    return [rows[i * CAND_BLOCK : (i + 1) * CAND_BLOCK] for i in range(count)], [None] * count


def scatter_sums(pieces, block_masks):
    if block_masks[0] is None:
        rows = jnp.concatenate(pieces, axis=0)
        return [lax.psum_scatter(rows, "seq", scatter_dimension=0, tiled=True)]
    own, near, far, both = pieces
    passed = swapped(both, "seq", 1)
    far = (far + passed.astype(jnp.float32)).astype(jnp.bfloat16)
    return [own, swapped(near, "seq", 1), swapped(far, "seq", 2)]


def on_device(candidates, gate_values, hist_keys, hist_values, pattern):
    hists = []
    for heads in CHUNKS:
        columns = slice(heads[0] * HEAD_DIM, (heads[-1] + 1) * HEAD_DIM)
        hists.append(jnp.concatenate([hist_keys[:, columns], hist_values[:, columns]], axis=1))
    across = [swapped(hist, "blk", 2) for hist in hists]
    rows, block_masks = gather_rows(candidates[0])
    beside = [swapped(hist, "blk", 1) for hist in hists]
    pieces = []
    for i, heads in enumerate(CHUNKS):
        kinds = [jnp.float32, jnp.bfloat16, jnp.float32, jnp.bfloat16]
        if block_masks[0] is None:
            kinds = [jnp.float32] * len(rows)
        start = attend(pattern, rows, [hists[i], beside[i]], heads, block_masks, [0, 1])
        diagonal = swapped(across[i], "blk", 1)
        sums = attend(
            pattern, rows, [across[i], diagonal], heads, block_masks, [2, 3], start, kinds
        )
        pieces.append(scatter_sums(sums, block_masks))
    return finish(gate_values[0], pieces)[None]


def solution(mesh):
    in_specs = (
        P(("groups", "blk"), "seq", None),
        P(("groups", "blk"), "seq", None),
        P(("groups", "seq", "blk"), None),
        P(("groups", "seq", "blk"), None),
        P("groups", None),
    )
    out_specs = P(("groups", "blk"), "seq", None)
    return jax.shard_map(
        on_device, mesh=mesh, in_specs=in_specs, out_specs=out_specs, check_vma=False
    )
```

```python
import functools

import jax
import jax.numpy as jnp
from jax import lax
from jax.experimental import pallas as pl
from jax.experimental.pallas import tpu as pltpu
from jax.sharding import PartitionSpec as P

HEADS = 4
HEAD_DIM = 128
CAND_BLOCK = 128
HALF_SCALE = 0.5 * HEAD_DIM ** (-0.5)
LONG = 10**10
PAIR = 2 * HEAD_DIM
VMEM_LIMIT = 48 * 1024 * 1024
PARAMS = pltpu.CompilerParams(vmem_limit_bytes=VMEM_LIMIT)
COST = pl.CostEstimate(flops=1, transcendentals=0, bytes_accessed=1)
VMEM = pl.BlockSpec(memory_space=pltpu.VMEM)


def swapped(block, axis, mask):
    size = lax.axis_size(axis)
    return lax.ppermute(block, axis, [(i, i ^ mask) for i in range(size)])


def after(block, *others):
    return lax.optimization_barrier((block, *others))[0]


def pack_kernel(queries, keys, values, *refs):
    outs, sems = refs[:-1], refs[-1]
    kept_queries, sent_queries, kept, sent = outs[0], outs[1], outs[2:6], outs[6:8]
    core = lax.rem(lax.axis_index("blk"), 2)
    count = keys.shape[0]
    copies = []

    def copy(source, target):
        copies.append(pltpu.make_async_copy(source, target, sems.at[len(copies)]))
        copies[-1].start()

    def columns(side, at, width):
        return pl.ds(pl.multiple_of(side * PAIR + at * HEAD_DIM, HEAD_DIM), width)

    copy(queries.at[:, columns(1 - core, 0, PAIR)], sent_queries)
    copy(queries.at[:, columns(core, 0, PAIR)], kept_queries)
    for at in range(2):
        copy(keys.at[:, columns(1 - core, at, HEAD_DIM)], sent[at].at[:count])
        copy(values.at[:, columns(1 - core, at, HEAD_DIM)], sent[at].at[count:])
        copy(keys.at[:, columns(core, at, HEAD_DIM)], kept[2 * at])
        copy(values.at[:, columns(core, at, HEAD_DIM)], kept[2 * at + 1])
    for each in copies:
        each.wait()


def pack(queries, keys, values):
    row_shape = jax.ShapeDtypeStruct((queries.shape[0], PAIR), queries.dtype)
    hist_shape = jax.ShapeDtypeStruct((keys.shape[0], HEAD_DIM), keys.dtype)
    sent_shape = jax.ShapeDtypeStruct((2 * keys.shape[0], HEAD_DIM), keys.dtype)
    return pl.pallas_call(
        pack_kernel,
        out_shape=[row_shape] * 2 + [hist_shape] * 4 + [sent_shape] * 2,
        in_specs=[pl.BlockSpec(memory_space=pltpu.HBM)] * 3,
        out_specs=[VMEM] * 8,
        scratch_shapes=[pltpu.SemaphoreType.DMA((10,))],
        compiler_params=PARAMS,
        cost_estimate=COST,
    )(*(pltpu.with_memory_space_constraint(x, pltpu.HBM) for x in (queries, keys, values)))


def weigh(pattern_ref, queries, keys, places, columns):
    events = keys.shape[0] // len(columns)
    scores = lax.dot_general(
        queries, keys, (((1,), (1,)), ((), ())), preferred_element_type=jnp.float32
    )
    rows = []
    for i, place in enumerate(places):
        weights = []
        for j, column in enumerate(columns):
            scale = pattern_ref[place, column].astype(jnp.float32) * HALF_SCALE
            half = scores[
                i * CAND_BLOCK : (i + 1) * CAND_BLOCK, j * events : (j + 1) * events
            ] * scale
            weights.append((half + half * jnp.tanh(half)).astype(jnp.bfloat16))
        rows.append(jnp.concatenate(weights, axis=1))
    return jnp.concatenate(rows, axis=0)


def mix(weights, values):
    return jnp.dot(weights, values, preferred_element_type=jnp.float32)


def head_rows(refs, head):
    wide = slice(head * HEAD_DIM, (head + 1) * HEAD_DIM)
    return jnp.concatenate([ref[:, wide] for ref in refs], axis=0)


def row_places(masks):
    seq, blk = lax.axis_index("seq"), lax.axis_index("blk")
    return [
        (blk ^ side) * lax.axis_size("seq") + (seq ^ mask) for mask in masks for side in (0, 1)
    ]


def hist_places(masks):
    seq, blk = lax.axis_index("seq"), lax.axis_index("blk")
    return [seq * lax.axis_size("blk") + (blk ^ mask) for mask in masks]


def early_kernel(pattern, own, near, far, *refs):
    for head in range(2):
        keys, values, out = refs[2 * head], refs[2 * head + 1], refs[4 + head]
        weights = weigh(
            pattern, head_rows((own, near, far), head), keys[...], row_places((0, 1, 2)), hist_places((0, 1))
        )
        out[...] = mix(weights, values[...])


def first_kernel(pattern, own, near, far, both, keys, values, far_hist, start, *outs):
    weights = weigh(pattern, head_rows((both,), 0), keys[...], row_places((3,)), hist_places((0, 1)))
    rest = mix(weights, values[...])
    events = keys.shape[0]
    weights = weigh(
        pattern, head_rows((own, near, far, both), 0), far_hist[:events], row_places(range(4)), hist_places((2, 3))
    )
    total = mix(weights, far_hist[events:]) + jnp.concatenate([start[...], rest], axis=0)
    near_own, near_far, sent = outs
    half = near_own.shape[0]
    near_own[...] = total[:half]
    near_far[...] = total[2 * half : 3 * half]
    sent[:half] = total[half : 2 * half].astype(sent.dtype)
    sent[half:] = total[3 * half :].astype(sent.dtype)


def weights_kernel(pattern, own, near, far, both, keys, values, far_next, rest, out):
    weights = weigh(pattern, head_rows((both,), 1), keys[...], row_places((3,)), hist_places((0, 1)))
    rest[...] = mix(weights, values[...])
    out[...] = weigh(
        pattern, head_rows((own, near, far, both), 1), far_next[: keys.shape[0]], row_places(range(4)), hist_places((2, 3))
    )


def second_kernel(weights, far_next, far_last, start, rest, *outs):
    events = far_last.shape[0]
    far_values = jnp.concatenate([far_next[2 * events :], far_last[...]], axis=0)
    total = mix(weights[...], far_values)
    total = total + jnp.concatenate([start[...], rest[...]], axis=0)
    own, others, theirs = outs
    count = own.shape[0]
    own[...] = total[:count]
    for i in range(4):
        at = 2 * i * count
        if i:
            others[(i - 1) * count : i * count] = total[at : at + count].astype(others.dtype)
        theirs[i * count : (i + 1) * count] = total[at + count : at + 2 * count].astype(theirs.dtype)


def call(kernel, outs, *inputs, flops=1):
    return pl.pallas_call(
        kernel,
        out_shape=[jax.ShapeDtypeStruct(shape, kind) for shape, kind in outs],
        in_specs=[
            pl.BlockSpec(memory_space=pltpu.SMEM) if x.dtype == jnp.int32 else VMEM for x in inputs
        ],
        out_specs=[VMEM] * len(outs),
        compiler_params=PARAMS,
        cost_estimate=pl.CostEstimate(flops=flops, transcendentals=0, bytes_accessed=1),
    )(*inputs)


def finish_kernel(gate_ref, first_mine, first_theirs, own, other, *refs):
    passed, out_ref = refs[:-1], refs[-1]
    core = lax.rem(lax.axis_index("blk"), 2)
    mine, theirs = own[...], other[...].astype(jnp.float32)
    for piece in passed:
        mine = mine + piece[:, :HEAD_DIM].astype(jnp.float32)
        theirs = theirs + piece[:, HEAD_DIM:].astype(jnp.float32)
    mine = jnp.concatenate([first_mine[...], mine], axis=1)
    theirs = jnp.concatenate([first_theirs[...], theirs], axis=1)
    squares = jnp.sum(mine * mine, axis=1, keepdims=True)
    squares = squares + jnp.sum(theirs * theirs, axis=1, keepdims=True)
    factor = lax.rsqrt(squares / (HEADS * HEAD_DIM) + 1e-05)
    first = jnp.where(core == 0, mine, theirs) * factor
    second = jnp.where(core == 0, theirs, mine) * factor
    gate = gate_ref[...].astype(jnp.float32)
    out_ref[:, :PAIR] = (first * gate[:, :PAIR]).astype(out_ref.dtype)
    out_ref[:, PAIR:] = (second * gate[:, PAIR:]).astype(out_ref.dtype)


def paired(candidates, gate_values, hist_keys, hist_values, pattern):
    count = CAND_BLOCK
    half = 2 * count
    events = hist_keys.shape[0]
    own, queries, *hists = pack(candidates[0], hist_keys, hist_values)
    beside = [swapped(hist, "blk", 1) for hist in hists[4:]]
    own = jnp.concatenate([own, swapped(queries, "blk", 1)], axis=0)
    keys, values = [], []
    for i in range(2):
        keys.append(jnp.concatenate([hists[2 * i], beside[i][:events]], axis=0))
        values.append(jnp.concatenate([hists[2 * i + 1], beside[i][events:]], axis=0))
    hist = jnp.concatenate([keys[0], values[0]], axis=0)
    far_hist = swapped(hist, "blk", 2)
    hist_next = jnp.concatenate([keys[1], values[1][:events]], axis=0)
    far_next = swapped(hist_next, "blk", 2)
    far_last = swapped(values[1][events:], "blk", 2)
    own = after(own, hist, hist_next)
    far = swapped(own, "seq", 2)
    near = swapped(own, "seq", 1)
    both = swapped(far, "seq", 1)

    f32, b16 = jnp.float32, jnp.bfloat16
    part = ((3 * half, HEAD_DIM), f32)
    early = call(
        early_kernel, [part, part], pattern, own, near, far, keys[0], values[0], keys[1], values[1]
    )
    outs = [((half, HEAD_DIM), f32), ((half, HEAD_DIM), f32), ((2 * half, HEAD_DIM), b16)]
    first = call(
        first_kernel, outs, pattern, own, near, far, both, keys[0], values[0], far_hist, early[0]
    )
    passed = swapped(first[2], "seq", 1)
    left, weights = call(
        weights_kernel,
        [((half, HEAD_DIM), f32), ((4 * half, 2 * events), b16)],
        pattern, own, near, far, both, after(keys[1], first[2]), values[1], far_next,
        flops=LONG,
    )
    folded = after(first[1], left) + passed[half:].astype(f32)
    last = swapped(folded.astype(b16), "seq", 2)
    first = first[0] + passed[:half].astype(f32) + last.astype(f32)
    first_theirs = swapped(first[count:], "blk", 1)

    outs = [((count, HEAD_DIM), f32), ((3 * count, HEAD_DIM), b16), ((4 * count, HEAD_DIM), b16)]
    own, others, theirs = call(second_kernel, outs, weights, far_next, far_last, early[1], left)
    came = swapped(theirs, "blk", 1)
    pieces = []
    for mask in (3, 2, 1):
        mine = others[(mask - 1) * count : mask * count]
        piece = jnp.concatenate([mine, came[mask * count : (mask + 1) * count]], axis=1)
        if mask == 1:
            piece, first_theirs = lax.optimization_barrier((piece, first_theirs))
        pieces.append(swapped(piece, "seq", mask))
    gate = gate_values[0]
    inputs = [gate, first[:count], first_theirs, own, came[:count], *pieces]
    return call(finish_kernel, [(gate.shape, gate.dtype)], *inputs)[0][None]


def general_kernel(places, pattern, rows, *refs):
    hists, out = refs[:-1], refs[-1]
    blk = lax.axis_index("blk")
    total = None
    for at, hist in enumerate(hists):
        weights = weigh(
            pattern, rows[...], hist[:, :HEAD_DIM], places(blk), hist_places((at,))
        )
        mixed = mix(weights, hist[:, HEAD_DIM:])
        total = mixed if total is None else total + mixed
    out[...] = total


def general_finish_kernel(gate_ref, *refs):
    sums, out_ref = refs[:-1], refs[-1]
    summed = jnp.concatenate([ref[...] for ref in sums], axis=1)
    mean_square = jnp.mean(summed * summed, axis=1, keepdims=True)
    normed = summed * lax.rsqrt(mean_square + 1e-05)
    out_ref[...] = (normed * gate_ref[...].astype(jnp.float32)).astype(out_ref.dtype)


def general(candidates, gate_values, hist_keys, hist_values, pattern):
    hists = []
    for head in range(HEADS):
        wide = slice(head * HEAD_DIM, (head + 1) * HEAD_DIM)
        hists.append(jnp.concatenate([hist_keys[:, wide], hist_values[:, wide]], axis=1))
    gathered = lax.all_gather(candidates[0], "seq", axis=0, tiled=True)
    blocks = gathered.shape[0] // CAND_BLOCK
    masks = range(lax.axis_size("blk"))

    def places(blk):
        return [blk * blocks + i for i in range(blocks)]

    sums = []
    for head in range(HEADS):
        wide = slice(head * HEAD_DIM, (head + 1) * HEAD_DIM)
        around = [swapped(hists[head], "blk", mask) if mask else hists[head] for mask in masks]
        outs = [((gathered.shape[0], HEAD_DIM), jnp.float32)]
        kernel = functools.partial(general_kernel, places)
        (total,) = call(kernel, outs, pattern, gathered[:, wide], *around)
        sums.append(lax.psum_scatter(total, "seq", scatter_dimension=0, tiled=True))
    return pl.pallas_call(
        general_finish_kernel,
        out_shape=jax.ShapeDtypeStruct(gate_values[0].shape, gate_values.dtype),
        in_specs=[VMEM] * (1 + HEADS),
        out_specs=VMEM,
    )(gate_values[0], *sums)[None]


def on_device(candidates, *others):
    if lax.axis_size("seq") == 4 and candidates.shape[1] == CAND_BLOCK:
        return paired(candidates, *others)
    return general(candidates, *others)


def solution(mesh):
    in_specs = (
        P(("groups", "blk"), "seq", None),
        P(("groups", "blk"), "seq", None),
        P(("groups", "seq", "blk"), None),
        P(("groups", "seq", "blk"), None),
        P("groups", None),
    )
    out_specs = P(("groups", "blk"), "seq", None)
    return jax.shard_map(
        on_device, mesh=mesh, in_specs=in_specs, out_specs=out_specs, check_vma=False
    )
```

```python
import functools

import jax
import jax.numpy as jnp
from jax import lax
from jax.experimental import pallas as pl
from jax.experimental.pallas import tpu as pltpu
from jax.sharding import PartitionSpec as P

HEADS = 4
HEAD_DIM = 128
CAND_BLOCK = 128
HALF_SCALE = 0.5 * HEAD_DIM ** (-0.5)
LONG = 10**10
PAIR = 2 * HEAD_DIM
VMEM_LIMIT = 48 * 1024 * 1024
PARAMS = pltpu.CompilerParams(vmem_limit_bytes=VMEM_LIMIT)
COST = pl.CostEstimate(flops=1, transcendentals=0, bytes_accessed=1)
VMEM = pl.BlockSpec(memory_space=pltpu.VMEM)


def swapped(block, axis, mask):
    size = lax.axis_size(axis)
    return lax.ppermute(block, axis, [(i, i ^ mask) for i in range(size)])


def after(block, *others):
    return lax.optimization_barrier((block, *others))[0]


def pack_kernel(queries, keys, values, *refs):
    outs, sems = refs[:-1], refs[-1]
    kept_queries, sent_queries, kept, sent = outs[0], outs[1], outs[2:4], outs[4:]
    core = lax.rem(lax.axis_index("blk"), 2)
    count = keys.shape[0]
    copies = []

    def copy(source, target):
        copies.append(pltpu.make_async_copy(source, target, sems.at[len(copies)]))
        copies[-1].start()

    def columns(side, at, width):
        return pl.ds(pl.multiple_of(side * PAIR + at * HEAD_DIM, HEAD_DIM), width)

    copy(queries.at[:, columns(1 - core, 0, PAIR)], sent_queries)
    copy(queries.at[:, columns(core, 0, PAIR)], kept_queries)
    targets = [part for block in sent for part in (block.at[:count], block.at[count:])]
    for at in range(2):
        copy(keys.at[:, columns(core, at, HEAD_DIM)], kept[at].at[:count])
        copy(values.at[:, columns(core, at, HEAD_DIM)], kept[at].at[count:])
        copy(keys.at[:, columns(1 - core, at, HEAD_DIM)], targets[2 * at])
        copy(values.at[:, columns(1 - core, at, HEAD_DIM)], targets[2 * at + 1])
    for each in copies:
        each.wait()


def pack(queries, keys, values):
    row_shape = jax.ShapeDtypeStruct((queries.shape[0], PAIR), queries.dtype)
    both_shape = jax.ShapeDtypeStruct((2 * keys.shape[0], HEAD_DIM), keys.dtype)
    return pl.pallas_call(
        pack_kernel,
        out_shape=[row_shape] * 2 + [both_shape] * 4,
        in_specs=[pl.BlockSpec(memory_space=pltpu.HBM)] * 3,
        out_specs=[VMEM] * 6,
        scratch_shapes=[pltpu.SemaphoreType.DMA((10,))],
        compiler_params=PARAMS,
        cost_estimate=COST,
    )(*(pltpu.with_memory_space_constraint(x, pltpu.HBM) for x in (queries, keys, values)))


def weigh(pattern_ref, queries, keys, places, columns):
    events = keys.shape[0] // len(columns)
    scores = lax.dot_general(
        queries, keys, (((1,), (1,)), ((), ())), preferred_element_type=jnp.float32
    )
    rows = []
    for i, place in enumerate(places):
        weights = []
        for j, column in enumerate(columns):
            scale = pattern_ref[place, column].astype(jnp.float32) * HALF_SCALE
            half = scores[
                i * CAND_BLOCK : (i + 1) * CAND_BLOCK, j * events : (j + 1) * events
            ] * scale
            weights.append((half + half * jnp.tanh(half)).astype(jnp.bfloat16))
        rows.append(jnp.concatenate(weights, axis=1))
    return jnp.concatenate(rows, axis=0)


def mix(weights, values):
    return jnp.dot(weights, values, preferred_element_type=jnp.float32)


def head_rows(refs, head):
    wide = slice(head * HEAD_DIM, (head + 1) * HEAD_DIM)
    return jnp.concatenate([ref[:, wide] for ref in refs], axis=0)


def row_places(masks):
    seq, blk = lax.axis_index("seq"), lax.axis_index("blk")
    return [
        (blk ^ side) * lax.axis_size("seq") + (seq ^ mask) for mask in masks for side in (0, 1)
    ]


def hist_places(masks):
    seq, blk = lax.axis_index("seq"), lax.axis_index("blk")
    return [seq * lax.axis_size("blk") + (blk ^ mask) for mask in masks]


def joined(hists):
    events = hists[0].shape[0] // 2
    keys = jnp.concatenate([hist[:events] for hist in hists], axis=0)
    return keys, jnp.concatenate([hist[events:] for hist in hists], axis=0)


def sums_kernel(head, row_masks, hist_masks, pattern, *refs):
    rows, refs = refs[: len(row_masks)], refs[len(row_masks) :]
    hists, refs = refs[: len(hist_masks)], refs[len(hist_masks) :]
    keys, values = joined(hists)
    weights = weigh(
        pattern, head_rows(rows, head), keys, row_places(row_masks), hist_places(hist_masks)
    )
    total = mix(weights, values)
    if refs[0].shape == total.shape and len(refs) > 1:
        total, refs = total + refs[0][...], refs[1:]
    done = 0
    for out in refs:
        out[...] = total[done : done + out.shape[0]].astype(out.dtype)
        done += out.shape[0]


def both_kernel(pattern, both, kept, beside, straight, diagonal, far_sums, out):
    half = far_sums.shape[0]
    keys, values = joined((kept, beside, straight, diagonal))
    weights = weigh(pattern, head_rows((both,), 0), keys, row_places((3,)), hist_places(range(4)))
    out[:half] = far_sums[...]
    out[half:] = mix(weights, values).astype(out.dtype)


def weights_kernel(pattern, own, near, far, both, kept, beside, straight, start, out):
    rows = head_rows((own, near, far, both), 1)
    keys, values = joined((kept, beside))
    weights = weigh(pattern, rows, keys, row_places(range(4)), hist_places((0, 1)))
    start[...] = mix(weights, values)
    events = straight.shape[0] // 2
    out[...] = weigh(pattern, rows, straight[:events], row_places(range(4)), hist_places((2,)))


def second_kernel(pattern, own, near, far, both, straight, diagonal, weights, start, *outs):
    rows = head_rows((own, near, far, both), 1)
    events = straight.shape[0] // 2
    late = weigh(pattern, rows, diagonal[:events], row_places(range(4)), hist_places((3,)))
    values = jnp.concatenate([straight[events:], diagonal[events:]], axis=0)
    total = mix(jnp.concatenate([weights[...], late], axis=1), values) + start[...]
    own, others, theirs = outs
    count = own.shape[0]
    own[...] = total[:count]
    for i in range(4):
        at = 2 * i * count
        if i:
            others[(i - 1) * count : i * count] = total[at : at + count].astype(others.dtype)
        theirs[i * count : (i + 1) * count] = total[at + count : at + 2 * count].astype(theirs.dtype)


def call(kernel, outs, *inputs, flops=1):
    return pl.pallas_call(
        kernel,
        out_shape=[jax.ShapeDtypeStruct(shape, kind) for shape, kind in outs],
        in_specs=[
            pl.BlockSpec(memory_space=pltpu.SMEM) if x.dtype == jnp.int32 else VMEM for x in inputs
        ],
        out_specs=[VMEM] * len(outs),
        compiler_params=PARAMS,
        cost_estimate=pl.CostEstimate(flops=flops, transcendentals=0, bytes_accessed=1),
    )(*inputs)


def finish_kernel(gate_ref, first_mine, first_theirs, own, other, *refs):
    passed, out_ref = refs[:-1], refs[-1]
    core = lax.rem(lax.axis_index("blk"), 2)
    mine, theirs = own[...], other[...].astype(jnp.float32)
    for piece in passed:
        mine = mine + piece[:, :HEAD_DIM].astype(jnp.float32)
        theirs = theirs + piece[:, HEAD_DIM:].astype(jnp.float32)
    mine = jnp.concatenate([first_mine[...], mine], axis=1)
    theirs = jnp.concatenate([first_theirs[...], theirs], axis=1)
    squares = jnp.sum(mine * mine, axis=1, keepdims=True)
    squares = squares + jnp.sum(theirs * theirs, axis=1, keepdims=True)
    factor = lax.rsqrt(squares / (HEADS * HEAD_DIM) + 1e-05)
    first = jnp.where(core == 0, mine, theirs) * factor
    second = jnp.where(core == 0, theirs, mine) * factor
    gate = gate_ref[...].astype(jnp.float32)
    out_ref[:, :PAIR] = (first * gate[:, :PAIR]).astype(out_ref.dtype)
    out_ref[:, PAIR:] = (second * gate[:, PAIR:]).astype(out_ref.dtype)


def paired(candidates, gate_values, hist_keys, hist_values, pattern):
    count = CAND_BLOCK
    half = 2 * count
    events = hist_keys.shape[0]
    own, queries, *hists = pack(candidates[0], hist_keys, hist_values)
    kept, sent = hists[:2], hists[2:]
    straight = [swapped(x, "blk", 2) for x in kept]
    diagonal = [swapped(x, "blk", 3) for x in sent]
    own = jnp.concatenate([own, swapped(queries, "blk", 1)], axis=0)
    beside = [swapped(x, "blk", 1) for x in sent]
    own = after(own, *beside)
    far = swapped(own, "seq", 2)
    near = swapped(own, "seq", 1)
    both = swapped(far, "seq", 1)

    f32, b16 = jnp.float32, jnp.bfloat16
    rows, three = (own, near, far, both), (own, near, far)
    part = ((half, HEAD_DIM), f32)
    early = call(
        functools.partial(sums_kernel, 0, (0, 1, 2), (0, 1)),
        [((3 * half, HEAD_DIM), f32)],
        pattern, *three, kept[0], beside[0],
    )
    first, first_near, sums = call(
        functools.partial(sums_kernel, 0, (0, 1, 2), (2, 3)),
        [part, part, ((half, HEAD_DIM), b16)],
        pattern, *three, straight[0], diagonal[0], *early,
    )
    (sums,) = call(
        both_kernel,
        [((2 * half, HEAD_DIM), b16)],
        pattern, both, kept[0], beside[0], straight[0], diagonal[0], sums,
    )
    passed = swapped(sums, "seq", 2)
    start, weights = call(
        weights_kernel,
        [((4 * half, HEAD_DIM), f32), ((4 * half, events), b16)],
        pattern, *rows, after(kept[1], sums), beside[1], straight[1],
        flops=LONG,
    )
    folded = first_near + passed[half:].astype(f32)
    last = swapped(folded.astype(b16), "seq", 1)
    first = first + passed[:half].astype(f32) + last.astype(f32)
    first_theirs = swapped(first[count:], "blk", 1)

    outs = [((count, HEAD_DIM), f32), ((3 * count, HEAD_DIM), b16), ((4 * count, HEAD_DIM), b16)]
    own, others, theirs = call(
        second_kernel, outs, pattern, *rows, straight[1], diagonal[1], weights, start, flops=LONG
    )
    came = swapped(theirs, "blk", 1)
    pieces = []
    for mask in (2, 3, 1):
        mine = others[(mask - 1) * count : mask * count]
        piece = jnp.concatenate([mine, came[mask * count : (mask + 1) * count]], axis=1)
        pieces.append(swapped(piece, "seq", mask))
    gate = gate_values[0]
    inputs = [gate, first[:count], first_theirs, own, came[:count], *pieces]
    return call(finish_kernel, [(gate.shape, gate.dtype)], *inputs)[0][None]


def general_kernel(places, pattern, rows, *refs):
    hists, out = refs[:-1], refs[-1]
    blk = lax.axis_index("blk")
    total = None
    for at, hist in enumerate(hists):
        weights = weigh(
            pattern, rows[...], hist[:, :HEAD_DIM], places(blk), hist_places((at,))
        )
        mixed = mix(weights, hist[:, HEAD_DIM:])
        total = mixed if total is None else total + mixed
    out[...] = total


def general_finish_kernel(gate_ref, *refs):
    sums, out_ref = refs[:-1], refs[-1]
    summed = jnp.concatenate([ref[...] for ref in sums], axis=1)
    mean_square = jnp.mean(summed * summed, axis=1, keepdims=True)
    normed = summed * lax.rsqrt(mean_square + 1e-05)
    out_ref[...] = (normed * gate_ref[...].astype(jnp.float32)).astype(out_ref.dtype)


def general(candidates, gate_values, hist_keys, hist_values, pattern):
    hists = []
    for head in range(HEADS):
        wide = slice(head * HEAD_DIM, (head + 1) * HEAD_DIM)
        hists.append(jnp.concatenate([hist_keys[:, wide], hist_values[:, wide]], axis=1))
    gathered = lax.all_gather(candidates[0], "seq", axis=0, tiled=True)
    blocks = gathered.shape[0] // CAND_BLOCK
    masks = range(lax.axis_size("blk"))

    def places(blk):
        return [blk * blocks + i for i in range(blocks)]

    sums = []
    for head in range(HEADS):
        wide = slice(head * HEAD_DIM, (head + 1) * HEAD_DIM)
        around = [swapped(hists[head], "blk", mask) if mask else hists[head] for mask in masks]
        outs = [((gathered.shape[0], HEAD_DIM), jnp.float32)]
        kernel = functools.partial(general_kernel, places)
        (total,) = call(kernel, outs, pattern, gathered[:, wide], *around)
        sums.append(lax.psum_scatter(total, "seq", scatter_dimension=0, tiled=True))
    return pl.pallas_call(
        general_finish_kernel,
        out_shape=jax.ShapeDtypeStruct(gate_values[0].shape, gate_values.dtype),
        in_specs=[VMEM] * (1 + HEADS),
        out_specs=VMEM,
    )(gate_values[0], *sums)[None]


def on_device(candidates, *others):
    if lax.axis_size("seq") == 4 and candidates.shape[1] == CAND_BLOCK:
        return paired(candidates, *others)
    return general(candidates, *others)


def solution(mesh):
    in_specs = (
        P(("groups", "blk"), "seq", None),
        P(("groups", "blk"), "seq", None),
        P(("groups", "seq", "blk"), None),
        P(("groups", "seq", "blk"), None),
        P("groups", None),
    )
    out_specs = P(("groups", "blk"), "seq", None)
    return jax.shard_map(
        on_device, mesh=mesh, in_specs=in_specs, out_specs=out_specs, check_vma=False
    )
```

```python
import functools

import jax
import jax.numpy as jnp
from jax import lax
from jax.experimental import pallas as pl
from jax.experimental.pallas import tpu as pltpu
from jax.sharding import PartitionSpec as P

HEADS = 4
HEAD_DIM = 128
CAND_BLOCK = 128
HALF_SCALE = 0.5 * HEAD_DIM ** (-0.5)
LONG = 10**10
PAIR = 2 * HEAD_DIM
ALONG = ((0, 0), (1, 0), (2, 0), (3, 0))
SQUARE = ((0, 0), (0, 2), (2, 0), (2, 2))
PAIRED = ((0, 0), (0, 1))
ACROSS = ((0, 2), (0, 3))
BESIDE = ((1, 0), (1, 1))
VMEM_LIMIT = 48 * 1024 * 1024
PARAMS = pltpu.CompilerParams(vmem_limit_bytes=VMEM_LIMIT)
COST = pl.CostEstimate(flops=1, transcendentals=0, bytes_accessed=1)
VMEM = pl.BlockSpec(memory_space=pltpu.VMEM)


def swapped(block, axis, mask):
    size = lax.axis_size(axis)
    return lax.ppermute(block, axis, [(i, i ^ mask) for i in range(size)])


def after(block, *others):
    return lax.optimization_barrier((block, *others))[0]


def pack_kernel(queries, keys, values, *refs):
    outs, sems = refs[:-1], refs[-1]
    kept_queries, sent_queries, kept, sent = outs[0], outs[1], outs[2:4], outs[4:]
    core = lax.rem(lax.axis_index("blk"), 2)
    count = keys.shape[0]
    copies = []

    def copy(source, target):
        copies.append(pltpu.make_async_copy(source, target, sems.at[len(copies)]))
        copies[-1].start()

    def columns(side, at, width):
        return pl.ds(pl.multiple_of(side * PAIR + at * HEAD_DIM, HEAD_DIM), width)

    copy(queries.at[:, columns(1 - core, 0, PAIR)], sent_queries)
    copy(queries.at[:, columns(core, 0, PAIR)], kept_queries)
    targets = [part for block in sent for part in (block.at[:count], block.at[count:])]
    for at in range(2):
        copy(keys.at[:, columns(core, at, HEAD_DIM)], kept[at].at[:count])
        copy(values.at[:, columns(core, at, HEAD_DIM)], kept[at].at[count:])
        copy(keys.at[:, columns(1 - core, at, HEAD_DIM)], targets[2 * at])
        copy(values.at[:, columns(1 - core, at, HEAD_DIM)], targets[2 * at + 1])
    for each in copies:
        each.wait()


def pack(queries, keys, values):
    row_shape = jax.ShapeDtypeStruct((queries.shape[0], PAIR), queries.dtype)
    both_shape = jax.ShapeDtypeStruct((2 * keys.shape[0], HEAD_DIM), keys.dtype)
    return pl.pallas_call(
        pack_kernel,
        out_shape=[row_shape] * 2 + [both_shape] * 4,
        in_specs=[pl.BlockSpec(memory_space=pltpu.HBM)] * 3,
        out_specs=[VMEM] * 6,
        scratch_shapes=[pltpu.SemaphoreType.DMA((10,))],
        compiler_params=PARAMS,
        cost_estimate=COST,
    )(*(pltpu.with_memory_space_constraint(x, pltpu.HBM) for x in (queries, keys, values)))


def weigh(pattern_ref, queries, keys, places, columns):
    events = keys.shape[0] // len(columns)
    scores = lax.dot_general(
        queries, keys, (((1,), (1,)), ((), ())), preferred_element_type=jnp.float32
    )
    rows = []
    for i, place in enumerate(places):
        weights = []
        for j, column in enumerate(columns):
            scale = pattern_ref[place, column].astype(jnp.float32) * HALF_SCALE
            half = scores[
                i * CAND_BLOCK : (i + 1) * CAND_BLOCK, j * events : (j + 1) * events
            ] * scale
            weights.append((half + half * jnp.tanh(half)).astype(jnp.bfloat16))
        rows.append(jnp.concatenate(weights, axis=1))
    return jnp.concatenate(rows, axis=0)


def mix(weights, values):
    return jnp.dot(weights, values, preferred_element_type=jnp.float32)


def head_rows(refs, head):
    wide = slice(head * HEAD_DIM, (head + 1) * HEAD_DIM)
    return jnp.concatenate(
        [ref[...] if ref.shape[1] == HEAD_DIM else ref[:, wide] for ref in refs], axis=0
    )


def row_places(places, sides=(0, 1)):
    seq, blk = lax.axis_index("seq"), lax.axis_index("blk")
    size = lax.axis_size("seq")
    return [(blk ^ across ^ side) * size + (seq ^ near) for near, across in places for side in sides]


def hist_places(places):
    seq, blk = lax.axis_index("seq"), lax.axis_index("blk")
    return [(seq ^ near) * lax.axis_size("blk") + (blk ^ across) for near, across in places]


def early_kernel(pattern, own, far, keys, values, out):
    rows = head_rows((own, far), 0)
    weights = weigh(pattern, rows, keys[...], row_places(ALONG[::2]), hist_places(PAIRED))
    out[...] = mix(weights, values[...])


def first_kernel(pattern, own, far, far_hist, start, own_out, far_out):
    half = own.shape[0]
    events = far_hist.shape[0] // 2
    rows = head_rows((own, far), 0)
    weights = weigh(pattern, rows, far_hist[:events], row_places(ALONG[::2]), hist_places(ACROSS))
    total = mix(weights, far_hist[events:]) + start[...]
    own_out[...] = total[:half]
    far_out[...] = total[half:]


def rest_kernel(pattern, near_pack, both, keys, values, far_hist, out):
    half = both.shape[0]
    events = keys.shape[0]
    rows = head_rows((near_pack.at[:half], both), 0)
    weights = weigh(pattern, rows, keys[...], row_places(ALONG[1::2]), hist_places(PAIRED))
    total = mix(weights, values[...])
    weights = weigh(pattern, rows, far_hist[:events], row_places(ALONG[1::2]), hist_places(ACROSS))
    out[...] = (total + mix(weights, far_hist[events:])).astype(out.dtype)


def weights_kernel(pattern, own, crosses, far, keys, values, near_pack, start, out):
    half = own.shape[0]
    rows = head_rows((own, crosses.at[:half], far, crosses.at[half:]), 1)
    weights = weigh(pattern, rows, keys[...], row_places(SQUARE), hist_places(PAIRED))
    start[...] = mix(weights, values[...])
    out[...] = weigh(pattern, rows, near_pack[half:], row_places(SQUARE), hist_places(BESIDE))


def second_kernel(weights, near_values, start, own, far, others):
    total = mix(weights[...], near_values[...]) + start[...]
    half = own.shape[0]
    own[...] = total[:half]
    far[...] = total[2 * half : 3 * half]
    others[:half] = total[half : 2 * half].astype(others.dtype)
    others[half:] = total[3 * half :].astype(others.dtype)


def call(kernel, outs, *inputs, flops=1):
    return pl.pallas_call(
        kernel,
        out_shape=[jax.ShapeDtypeStruct(shape, kind) for shape, kind in outs],
        in_specs=[
            pl.BlockSpec(memory_space=pltpu.SMEM) if x.dtype == jnp.int32 else VMEM for x in inputs
        ],
        out_specs=[VMEM] * len(outs),
        compiler_params=PARAMS,
        cost_estimate=pl.CostEstimate(flops=flops, transcendentals=0, bytes_accessed=1),
    )(*inputs)


def finish_kernel(gate_ref, first_mine, first_theirs, second_mine, second_theirs, out_ref):
    core = lax.rem(lax.axis_index("blk"), 2)
    mine = jnp.concatenate([first_mine[...], second_mine[...]], axis=1)
    theirs = jnp.concatenate([first_theirs[...], second_theirs[...]], axis=1)
    squares = jnp.sum(mine * mine, axis=1, keepdims=True)
    squares = squares + jnp.sum(theirs * theirs, axis=1, keepdims=True)
    factor = lax.rsqrt(squares / (HEADS * HEAD_DIM) + 1e-05)
    first = jnp.where(core == 0, mine, theirs) * factor
    second = jnp.where(core == 0, theirs, mine) * factor
    gate = gate_ref[...].astype(jnp.float32)
    out_ref[:, :PAIR] = (first * gate[:, :PAIR]).astype(out_ref.dtype)
    out_ref[:, PAIR:] = (second * gate[:, PAIR:]).astype(out_ref.dtype)


def reduced(own, far, others, axis, mask):
    half = own.shape[0]
    passed = swapped(others, axis, mask).astype(jnp.float32)
    last = swapped((far + passed[half:]).astype(others.dtype), "seq", 2)
    return own + passed[:half] + last.astype(jnp.float32)


def paired(candidates, gate_values, hist_keys, hist_values, pattern):
    count = CAND_BLOCK
    half = 2 * count
    events = hist_keys.shape[0]
    own, queries, *hists = pack(candidates[0], hist_keys, hist_values)
    kept, sent = hists[:2], hists[2:]
    own = jnp.concatenate([own, swapped(queries, "blk", 1)], axis=0)
    beside = [swapped(x, "blk", 1) for x in sent]
    keys = [jnp.concatenate([x[:events], y[:events]], axis=0) for x, y in zip(kept, beside)]
    values = [jnp.concatenate([x[events:], y[events:]], axis=0) for x, y in zip(kept, beside)]
    hist = jnp.concatenate([keys[0], values[0]], axis=0)
    own = after(own, hist)
    far = swapped(own, "seq", 2)
    far_hist = swapped(hist, "blk", 2)
    near_pack = swapped(jnp.concatenate([own[:, :HEAD_DIM], keys[1]], axis=0), "seq", 1)
    both = swapped(far[:, :HEAD_DIM], "seq", 1)
    near_values = swapped(after(values[1], far), "seq", 1)
    crosses = swapped(jnp.concatenate([own[:, HEAD_DIM:], far[:, HEAD_DIM:]], axis=0), "blk", 2)

    f32, b16 = jnp.float32, jnp.bfloat16
    part = ((half, HEAD_DIM), f32)
    (early,) = call(early_kernel, [((2 * half, HEAD_DIM), f32)], pattern, own, far, keys[0], values[0])
    first, first_far = call(first_kernel, [part, part], pattern, own, far, far_hist, early)
    start, weights = call(
        weights_kernel,
        [((4 * half, HEAD_DIM), f32), ((4 * half, 2 * events), b16)],
        pattern, own, crosses, far, after(keys[1], first), values[1], near_pack,
        flops=LONG,
    )
    (sums,) = call(
        rest_kernel,
        [((2 * half, HEAD_DIM), b16)],
        pattern, near_pack, both, after(keys[0], start), values[0], far_hist,
    )
    outs = [part, part, ((2 * half, HEAD_DIM), b16)]
    second, second_far, others = call(second_kernel, outs, weights, near_values, start)
    first, second = (
        reduced(*x) for x in ((first, first_far, sums, "seq", 1), (second, second_far, others, "blk", 2))
    )
    pieces = []
    for x in (first, second):
        pieces += [x[:count], swapped(x[count:], "blk", 1)]
    gate = gate_values[0]
    inputs = [gate, *pieces]
    return call(finish_kernel, [(gate.shape, gate.dtype)], *inputs)[0][None]


def general_kernel(places, pattern, rows, *refs):
    hists, out = refs[:-1], refs[-1]
    blk = lax.axis_index("blk")
    total = None
    for at, hist in enumerate(hists):
        weights = weigh(
            pattern, rows[...], hist[:, :HEAD_DIM], places(blk), hist_places(((0, at),))
        )
        mixed = mix(weights, hist[:, HEAD_DIM:])
        total = mixed if total is None else total + mixed
    out[...] = total


def general_finish_kernel(gate_ref, *refs):
    sums, out_ref = refs[:-1], refs[-1]
    summed = jnp.concatenate([ref[...] for ref in sums], axis=1)
    mean_square = jnp.mean(summed * summed, axis=1, keepdims=True)
    normed = summed * lax.rsqrt(mean_square + 1e-05)
    out_ref[...] = (normed * gate_ref[...].astype(jnp.float32)).astype(out_ref.dtype)


def general(candidates, gate_values, hist_keys, hist_values, pattern):
    hists = []
    for head in range(HEADS):
        wide = slice(head * HEAD_DIM, (head + 1) * HEAD_DIM)
        hists.append(jnp.concatenate([hist_keys[:, wide], hist_values[:, wide]], axis=1))
    gathered = lax.all_gather(candidates[0], "seq", axis=0, tiled=True)
    blocks = gathered.shape[0] // CAND_BLOCK
    masks = range(lax.axis_size("blk"))

    def places(blk):
        return [blk * blocks + i for i in range(blocks)]

    sums = []
    for head in range(HEADS):
        wide = slice(head * HEAD_DIM, (head + 1) * HEAD_DIM)
        around = [swapped(hists[head], "blk", mask) if mask else hists[head] for mask in masks]
        outs = [((gathered.shape[0], HEAD_DIM), jnp.float32)]
        kernel = functools.partial(general_kernel, places)
        (total,) = call(kernel, outs, pattern, gathered[:, wide], *around)
        sums.append(lax.psum_scatter(total, "seq", scatter_dimension=0, tiled=True))
    return pl.pallas_call(
        general_finish_kernel,
        out_shape=jax.ShapeDtypeStruct(gate_values[0].shape, gate_values.dtype),
        in_specs=[VMEM] * (1 + HEADS),
        out_specs=VMEM,
    )(gate_values[0], *sums)[None]


def on_device(candidates, *others):
    if lax.axis_size("seq") == 4 and candidates.shape[1] == CAND_BLOCK:
        return paired(candidates, *others)
    return general(candidates, *others)


def solution(mesh):
    in_specs = (
        P(("groups", "blk"), "seq", None),
        P(("groups", "blk"), "seq", None),
        P(("groups", "seq", "blk"), None),
        P(("groups", "seq", "blk"), None),
        P("groups", None),
    )
    out_specs = P(("groups", "blk"), "seq", None)
    return jax.shard_map(
        on_device, mesh=mesh, in_specs=in_specs, out_specs=out_specs, check_vma=False
    )
```

```python
import functools

import jax
import jax.numpy as jnp
from jax import lax
from jax.experimental import pallas as pl
from jax.experimental.pallas import tpu as pltpu
from jax.sharding import PartitionSpec as P

HEADS = 4
HEAD_DIM = 128
CAND_BLOCK = 128
HALF_SCALE = 0.5 * HEAD_DIM ** (-0.5)
LONG = 10**10
PAIR = 2 * HEAD_DIM
ALONG = ((0, 0), (1, 0), (2, 0), (3, 0))
SQUARE = ((0, 0), (0, 2), (2, 0), (2, 2))
PAIRED = ((0, 0), (0, 1))
ACROSS = ((0, 2), (0, 3))
BESIDE = ((1, 0), (1, 1))
VMEM_LIMIT = 48 * 1024 * 1024
PARAMS = pltpu.CompilerParams(vmem_limit_bytes=VMEM_LIMIT)
COST = pl.CostEstimate(flops=1, transcendentals=0, bytes_accessed=1)
VMEM = pl.BlockSpec(memory_space=pltpu.VMEM)


def swapped(block, axis, mask):
    size = lax.axis_size(axis)
    return lax.ppermute(block, axis, [(i, i ^ mask) for i in range(size)])


def after(block, *others):
    return lax.optimization_barrier((block, *others))[0]


def pack_kernel(queries, keys, values, *refs):
    outs, sems = refs[:-1], refs[-1]
    kept_queries, sent_queries, kept, sent = outs[0], outs[1], outs[2:4], outs[4:]
    core = lax.rem(lax.axis_index("blk"), 2)
    count = keys.shape[0]
    copies = []

    def copy(source, target):
        copies.append(pltpu.make_async_copy(source, target, sems.at[len(copies)]))
        copies[-1].start()

    def columns(side, at, width):
        return pl.ds(pl.multiple_of(side * PAIR + at * HEAD_DIM, HEAD_DIM), width)

    copy(queries.at[:, columns(1 - core, 0, PAIR)], sent_queries)
    copy(queries.at[:, columns(core, 0, PAIR)], kept_queries)
    targets = [part for block in sent for part in (block.at[:count], block.at[count:])]
    for at in range(2):
        copy(keys.at[:, columns(core, at, HEAD_DIM)], kept[at].at[:count])
        copy(values.at[:, columns(core, at, HEAD_DIM)], kept[at].at[count:])
        copy(keys.at[:, columns(1 - core, at, HEAD_DIM)], targets[2 * at])
        copy(values.at[:, columns(1 - core, at, HEAD_DIM)], targets[2 * at + 1])
    for each in copies:
        each.wait()


def pack(queries, keys, values):
    row_shape = jax.ShapeDtypeStruct((queries.shape[0], PAIR), queries.dtype)
    both_shape = jax.ShapeDtypeStruct((2 * keys.shape[0], HEAD_DIM), keys.dtype)
    return pl.pallas_call(
        pack_kernel,
        out_shape=[row_shape] * 2 + [both_shape] * 4,
        in_specs=[pl.BlockSpec(memory_space=pltpu.HBM)] * 3,
        out_specs=[VMEM] * 6,
        scratch_shapes=[pltpu.SemaphoreType.DMA((10,))],
        compiler_params=PARAMS,
        cost_estimate=COST,
    )(*(pltpu.with_memory_space_constraint(x, pltpu.HBM) for x in (queries, keys, values)))


def weigh(pattern_ref, queries, keys, places, columns):
    events = keys.shape[0] // len(columns)
    scores = lax.dot_general(
        queries, keys, (((1,), (1,)), ((), ())), preferred_element_type=jnp.float32
    )
    rows = []
    for i, place in enumerate(places):
        weights = []
        for j, column in enumerate(columns):
            scale = pattern_ref[place, column].astype(jnp.float32) * HALF_SCALE
            half = scores[
                i * CAND_BLOCK : (i + 1) * CAND_BLOCK, j * events : (j + 1) * events
            ] * scale
            weights.append((half + half * jnp.tanh(half)).astype(jnp.bfloat16))
        rows.append(jnp.concatenate(weights, axis=1))
    return jnp.concatenate(rows, axis=0)


def mix(weights, values):
    return jnp.dot(weights, values, preferred_element_type=jnp.float32)


def head_rows(refs, head):
    wide = slice(head * HEAD_DIM, (head + 1) * HEAD_DIM)
    return jnp.concatenate(
        [ref[...] if ref.shape[1] == HEAD_DIM else ref[:, wide] for ref in refs], axis=0
    )


def row_places(places, sides=(0, 1)):
    seq, blk = lax.axis_index("seq"), lax.axis_index("blk")
    size = lax.axis_size("seq")
    return [(blk ^ across ^ side) * size + (seq ^ near) for near, across in places for side in sides]


def hist_places(places):
    seq, blk = lax.axis_index("seq"), lax.axis_index("blk")
    return [(seq ^ near) * lax.axis_size("blk") + (blk ^ across) for near, across in places]


def early_kernel(pattern, own, far, keys, values, out):
    rows = head_rows((own, far), 0)
    weights = weigh(pattern, rows, keys[...], row_places(ALONG[::2]), hist_places(PAIRED))
    out[...] = mix(weights, values[...])


def first_kernel(pattern, own, far, far_hist, start, own_out, far_out):
    half = own.shape[0]
    events = far_hist.shape[0] // 2
    rows = head_rows((own, far), 0)
    weights = weigh(pattern, rows, far_hist[:events], row_places(ALONG[::2]), hist_places(ACROSS))
    total = mix(weights, far_hist[events:]) + start[...]
    own_out[...] = total[:half]
    far_out[...] = total[half:]


def rest_kernel(pattern, near_pack, both, keys, values, far_hist, out):
    half = both.shape[0]
    events = keys.shape[0]
    rows = head_rows((near_pack.at[:half], both), 0)
    weights = weigh(pattern, rows, keys[...], row_places(ALONG[1::2]), hist_places(PAIRED))
    total = mix(weights, values[...])
    weights = weigh(pattern, rows, far_hist[:events], row_places(ALONG[1::2]), hist_places(ACROSS))
    out[...] = (total + mix(weights, far_hist[events:])).astype(out.dtype)


def weights_kernel(pattern, own, crosses, far, keys, values, near_pack, start, out):
    half = own.shape[0]
    rows = head_rows((own, crosses.at[:half], far, crosses.at[half:]), 1)
    weights = weigh(pattern, rows, keys[...], row_places(SQUARE), hist_places(PAIRED))
    start[...] = mix(weights, values[...])
    out[...] = weigh(pattern, rows, near_pack[half:], row_places(SQUARE), hist_places(BESIDE))


def work_kernel(pattern, own, crosses, far, keys, values, near_pack, both, first_keys, first_values, far_hist, start, weights, out):
    weights_kernel(pattern, own, crosses, far, keys, values, near_pack, start, weights)
    rest_kernel(pattern, near_pack, both, first_keys, first_values, far_hist, out)


def second_kernel(weights, near_values, start, own, far, others):
    total = mix(weights[...], near_values[...]) + start[...]
    half = own.shape[0]
    own[...] = total[:half]
    far[...] = total[2 * half : 3 * half]
    others[:half] = total[half : 2 * half].astype(others.dtype)
    others[half:] = total[3 * half :].astype(others.dtype)


def call(kernel, outs, *inputs, flops=1):
    return pl.pallas_call(
        kernel,
        out_shape=[jax.ShapeDtypeStruct(shape, kind) for shape, kind in outs],
        in_specs=[
            pl.BlockSpec(memory_space=pltpu.SMEM) if x.dtype == jnp.int32 else VMEM for x in inputs
        ],
        out_specs=[VMEM] * len(outs),
        compiler_params=PARAMS,
        cost_estimate=pl.CostEstimate(flops=flops, transcendentals=0, bytes_accessed=1),
    )(*inputs)


def finish_kernel(gate_ref, first_mine, first_theirs, second_mine, second_theirs, out_ref):
    core = lax.rem(lax.axis_index("blk"), 2)
    mine = jnp.concatenate([first_mine[...], second_mine[...]], axis=1)
    theirs = jnp.concatenate([first_theirs[...], second_theirs[...]], axis=1)
    squares = jnp.sum(mine * mine, axis=1, keepdims=True)
    squares = squares + jnp.sum(theirs * theirs, axis=1, keepdims=True)
    factor = lax.rsqrt(squares / (HEADS * HEAD_DIM) + 1e-05)
    first = jnp.where(core == 0, mine, theirs) * factor
    second = jnp.where(core == 0, theirs, mine) * factor
    gate = gate_ref[...].astype(jnp.float32)
    out_ref[:, :PAIR] = (first * gate[:, :PAIR]).astype(out_ref.dtype)
    out_ref[:, PAIR:] = (second * gate[:, PAIR:]).astype(out_ref.dtype)


def reduced(own, far, others, axis, mask):
    half = own.shape[0]
    passed = swapped(others, axis, mask).astype(jnp.float32)
    last = swapped((far + passed[half:]).astype(others.dtype), "seq", 2)
    return own + passed[:half] + last.astype(jnp.float32)


def paired(candidates, gate_values, hist_keys, hist_values, pattern):
    count = CAND_BLOCK
    half = 2 * count
    events = hist_keys.shape[0]
    own, queries, *hists = pack(candidates[0], hist_keys, hist_values)
    kept, sent = hists[:2], hists[2:]
    own = jnp.concatenate([own, swapped(queries, "blk", 1)], axis=0)
    beside = [swapped(x, "blk", 1) for x in sent]
    keys = [jnp.concatenate([x[:events], y[:events]], axis=0) for x, y in zip(kept, beside)]
    values = [jnp.concatenate([x[events:], y[events:]], axis=0) for x, y in zip(kept, beside)]
    hist = jnp.concatenate([keys[0], values[0]], axis=0)
    own = after(own, hist)
    far = swapped(own, "seq", 2)
    far_hist = swapped(hist, "blk", 2)
    near_pack = swapped(jnp.concatenate([own[:, :HEAD_DIM], keys[1]], axis=0), "seq", 1)
    both = swapped(far[:, :HEAD_DIM], "seq", 1)
    near_values = swapped(after(values[1], far), "seq", 1)
    crosses = swapped(jnp.concatenate([own[:, HEAD_DIM:], far[:, HEAD_DIM:]], axis=0), "blk", 2)

    f32, b16 = jnp.float32, jnp.bfloat16
    part = ((half, HEAD_DIM), f32)
    (early,) = call(early_kernel, [((2 * half, HEAD_DIM), f32)], pattern, own, far, keys[0], values[0])
    first, first_far = call(first_kernel, [part, part], pattern, own, far, far_hist, early)
    start, weights, sums = call(
        work_kernel,
        [((4 * half, HEAD_DIM), f32), ((4 * half, 2 * events), b16), ((2 * half, HEAD_DIM), b16)],
        pattern, own, crosses, far, after(keys[1], first), values[1], near_pack, both, keys[0], values[0], far_hist,
        flops=LONG,
    )
    outs = [part, part, ((2 * half, HEAD_DIM), b16)]
    second, second_far, others = call(second_kernel, outs, weights, near_values, start, flops=LONG)
    first, second = (
        reduced(*x) for x in ((first, first_far, sums, "seq", 1), (second, second_far, others, "blk", 2))
    )
    pieces = []
    for x in (first, second):
        pieces += [x[:count], swapped(x[count:], "blk", 1)]
    gate = gate_values[0]
    inputs = [gate, *pieces]
    return call(finish_kernel, [(gate.shape, gate.dtype)], *inputs)[0][None]


def general_kernel(places, pattern, rows, *refs):
    hists, out = refs[:-1], refs[-1]
    blk = lax.axis_index("blk")
    total = None
    for at, hist in enumerate(hists):
        weights = weigh(
            pattern, rows[...], hist[:, :HEAD_DIM], places(blk), hist_places(((0, at),))
        )
        mixed = mix(weights, hist[:, HEAD_DIM:])
        total = mixed if total is None else total + mixed
    out[...] = total


def general_finish_kernel(gate_ref, *refs):
    sums, out_ref = refs[:-1], refs[-1]
    summed = jnp.concatenate([ref[...] for ref in sums], axis=1)
    mean_square = jnp.mean(summed * summed, axis=1, keepdims=True)
    normed = summed * lax.rsqrt(mean_square + 1e-05)
    out_ref[...] = (normed * gate_ref[...].astype(jnp.float32)).astype(out_ref.dtype)


def general(candidates, gate_values, hist_keys, hist_values, pattern):
    hists = []
    for head in range(HEADS):
        wide = slice(head * HEAD_DIM, (head + 1) * HEAD_DIM)
        hists.append(jnp.concatenate([hist_keys[:, wide], hist_values[:, wide]], axis=1))
    gathered = lax.all_gather(candidates[0], "seq", axis=0, tiled=True)
    blocks = gathered.shape[0] // CAND_BLOCK
    masks = range(lax.axis_size("blk"))

    def places(blk):
        return [blk * blocks + i for i in range(blocks)]

    sums = []
    for head in range(HEADS):
        wide = slice(head * HEAD_DIM, (head + 1) * HEAD_DIM)
        around = [swapped(hists[head], "blk", mask) if mask else hists[head] for mask in masks]
        outs = [((gathered.shape[0], HEAD_DIM), jnp.float32)]
        kernel = functools.partial(general_kernel, places)
        (total,) = call(kernel, outs, pattern, gathered[:, wide], *around)
        sums.append(lax.psum_scatter(total, "seq", scatter_dimension=0, tiled=True))
    return pl.pallas_call(
        general_finish_kernel,
        out_shape=jax.ShapeDtypeStruct(gate_values[0].shape, gate_values.dtype),
        in_specs=[VMEM] * (1 + HEADS),
        out_specs=VMEM,
    )(gate_values[0], *sums)[None]


def on_device(candidates, *others):
    if lax.axis_size("seq") == 4 and candidates.shape[1] == CAND_BLOCK:
        return paired(candidates, *others)
    return general(candidates, *others)


def solution(mesh):
    in_specs = (
        P(("groups", "blk"), "seq", None),
        P(("groups", "blk"), "seq", None),
        P(("groups", "seq", "blk"), None),
        P(("groups", "seq", "blk"), None),
        P("groups", None),
    )
    out_specs = P(("groups", "blk"), "seq", None)
    return jax.shard_map(
        on_device, mesh=mesh, in_specs=in_specs, out_specs=out_specs, check_vma=False
    )
```

```python
import functools

import jax
import jax.numpy as jnp
from jax import lax
from jax.experimental import pallas as pl
from jax.experimental.pallas import tpu as pltpu
from jax.sharding import PartitionSpec as P

HEADS = 4
HEAD_DIM = 128
CAND_BLOCK = 128
HALF_SCALE = 0.5 * HEAD_DIM ** (-0.5)
LONG = 10**10
PAIR = 2 * HEAD_DIM
ALONG = ((0, 0), (1, 0), (2, 0), (3, 0))
SQUARE = ((0, 0), (0, 2), (2, 0), (2, 2))
PAIRED = ((0, 0), (0, 1))
ACROSS = ((0, 2), (0, 3))
BESIDE = ((1, 0), (1, 1))
VMEM_LIMIT = 48 * 1024 * 1024
PARAMS = pltpu.CompilerParams(vmem_limit_bytes=VMEM_LIMIT)
COST = pl.CostEstimate(flops=1, transcendentals=0, bytes_accessed=1)
VMEM = pl.BlockSpec(memory_space=pltpu.VMEM)


def swapped(block, axis, mask):
    size = lax.axis_size(axis)
    return lax.ppermute(block, axis, [(i, i ^ mask) for i in range(size)])


def after(block, *others):
    return lax.optimization_barrier((block, *others))[0]


def pack_kernel(queries, keys, values, *refs):
    outs, sems = refs[:-1], refs[-1]
    kept_queries, sent_queries, kept, sent = outs[0], outs[1], outs[2:4], outs[4:]
    core = lax.rem(lax.axis_index("blk"), 2)
    count = keys.shape[0]
    copies = []

    def copy(source, target):
        copies.append(pltpu.make_async_copy(source, target, sems.at[len(copies)]))
        copies[-1].start()

    def columns(side, at, width):
        return pl.ds(pl.multiple_of(side * PAIR + at * HEAD_DIM, HEAD_DIM), width)

    copy(queries.at[:, columns(1 - core, 0, PAIR)], sent_queries)
    copy(queries.at[:, columns(core, 0, PAIR)], kept_queries)
    targets = [part for block in sent for part in (block.at[:count], block.at[count:])]
    for at in range(2):
        copy(keys.at[:, columns(core, at, HEAD_DIM)], kept[at].at[:count])
        copy(values.at[:, columns(core, at, HEAD_DIM)], kept[at].at[count:])
        copy(keys.at[:, columns(1 - core, at, HEAD_DIM)], targets[2 * at])
        copy(values.at[:, columns(1 - core, at, HEAD_DIM)], targets[2 * at + 1])
    for each in copies:
        each.wait()


def pack(queries, keys, values):
    row_shape = jax.ShapeDtypeStruct((queries.shape[0], PAIR), queries.dtype)
    both_shape = jax.ShapeDtypeStruct((2 * keys.shape[0], HEAD_DIM), keys.dtype)
    return pl.pallas_call(
        pack_kernel,
        out_shape=[row_shape] * 2 + [both_shape] * 4,
        in_specs=[pl.BlockSpec(memory_space=pltpu.HBM)] * 3,
        out_specs=[VMEM] * 6,
        scratch_shapes=[pltpu.SemaphoreType.DMA((10,))],
        compiler_params=PARAMS,
        cost_estimate=COST,
    )(*(pltpu.with_memory_space_constraint(x, pltpu.HBM) for x in (queries, keys, values)))


def weigh(pattern_ref, queries, keys, places, columns):
    events = keys.shape[0] // len(columns)
    scores = lax.dot_general(
        queries, keys, (((1,), (1,)), ((), ())), preferred_element_type=jnp.float32
    )
    rows = []
    for i, place in enumerate(places):
        weights = []
        for j, column in enumerate(columns):
            scale = pattern_ref[place, column].astype(jnp.float32) * HALF_SCALE
            half = scores[
                i * CAND_BLOCK : (i + 1) * CAND_BLOCK, j * events : (j + 1) * events
            ] * scale
            weights.append((half + half * jnp.tanh(half)).astype(jnp.bfloat16))
        rows.append(jnp.concatenate(weights, axis=1))
    return jnp.concatenate(rows, axis=0)


def mix(weights, values):
    return jnp.dot(weights, values, preferred_element_type=jnp.float32)


def head_rows(refs, head):
    wide = slice(head * HEAD_DIM, (head + 1) * HEAD_DIM)
    return jnp.concatenate(
        [ref[...] if ref.shape[1] == HEAD_DIM else ref[:, wide] for ref in refs], axis=0
    )


def row_places(places, sides=(0, 1)):
    seq, blk = lax.axis_index("seq"), lax.axis_index("blk")
    size = lax.axis_size("seq")
    return [(blk ^ across ^ side) * size + (seq ^ near) for near, across in places for side in sides]


def hist_places(places):
    seq, blk = lax.axis_index("seq"), lax.axis_index("blk")
    return [(seq ^ near) * lax.axis_size("blk") + (blk ^ across) for near, across in places]


def early_kernel(pattern, own, far, keys, values, out):
    rows = head_rows((own, far), 0)
    weights = weigh(pattern, rows, keys[...], row_places(ALONG[::2]), hist_places(PAIRED))
    out[...] = mix(weights, values[...])


def first_kernel(pattern, own, far, far_hist, start, own_out, far_out):
    half = own.shape[0]
    events = far_hist.shape[0] // 2
    rows = head_rows((own, far), 0)
    weights = weigh(pattern, rows, far_hist[:events], row_places(ALONG[::2]), hist_places(ACROSS))
    total = mix(weights, far_hist[events:]) + start[...]
    own_out[...] = total[:half]
    far_out[...] = total[half:]


def rest_kernel(pattern, near_pack, both, keys, values, far_hist, out):
    half = both.shape[0]
    events = keys.shape[0]
    rows = head_rows((near_pack.at[:half], both), 0)
    weights = weigh(pattern, rows, keys[...], row_places(ALONG[1::2]), hist_places(PAIRED))
    total = mix(weights, values[...])
    weights = weigh(pattern, rows, far_hist[:events], row_places(ALONG[1::2]), hist_places(ACROSS))
    out[...] = (total + mix(weights, far_hist[events:])).astype(out.dtype)


def weights_kernel(pattern, own, crosses, far, keys, values, near_pack, start, out):
    half = own.shape[0]
    rows = head_rows((own, crosses.at[:half], far, crosses.at[half:]), 1)
    weights = weigh(pattern, rows, keys[...], row_places(SQUARE), hist_places(PAIRED))
    start[...] = mix(weights, values[...])
    out[...] = weigh(pattern, rows, near_pack[half:], row_places(SQUARE), hist_places(BESIDE))


def work_kernel(pattern, own, crosses, far, keys, values, near_pack, both, first_keys, first_values, far_hist, start, weights, out):
    weights_kernel(pattern, own, crosses, far, keys, values, near_pack, start, weights)
    rest_kernel(pattern, near_pack, both, first_keys, first_values, far_hist, out)


def second_kernel(weights, near_values, start, own, far, others):
    total = mix(weights[...], near_values[...]) + start[...]
    half = own.shape[0]
    own[...] = total[:half]
    far[...] = total[2 * half : 3 * half]
    others[:half] = total[half : 2 * half].astype(others.dtype)
    others[half:] = total[3 * half :].astype(others.dtype)


def call(kernel, outs, *inputs, flops=1):
    return pl.pallas_call(
        kernel,
        out_shape=[jax.ShapeDtypeStruct(shape, kind) for shape, kind in outs],
        in_specs=[
            pl.BlockSpec(memory_space=pltpu.SMEM) if x.dtype == jnp.int32 else VMEM for x in inputs
        ],
        out_specs=[VMEM] * len(outs),
        compiler_params=PARAMS,
        cost_estimate=pl.CostEstimate(flops=flops, transcendentals=0, bytes_accessed=1),
    )(*inputs)


def finish_kernel(gate_ref, first_mine, first_theirs, second_mine, second_theirs, out_ref):
    core = lax.rem(lax.axis_index("blk"), 2)
    mine = jnp.concatenate([first_mine[...], second_mine[...]], axis=1)
    theirs = jnp.concatenate([first_theirs[...], second_theirs[...]], axis=1)
    squares = jnp.sum(mine * mine, axis=1, keepdims=True)
    squares = squares + jnp.sum(theirs * theirs, axis=1, keepdims=True)
    factor = lax.rsqrt(squares / (HEADS * HEAD_DIM) + 1e-05)
    first = jnp.where(core == 0, mine, theirs) * factor
    second = jnp.where(core == 0, theirs, mine) * factor
    gate = gate_ref[...].astype(jnp.float32)
    out_ref[:, :PAIR] = (first * gate[:, :PAIR]).astype(out_ref.dtype)
    out_ref[:, PAIR:] = (second * gate[:, PAIR:]).astype(out_ref.dtype)


def reduced(own, far, others, axis, mask):
    half = own.shape[0]
    passed = swapped(others, axis, mask).astype(jnp.float32)
    last = swapped((far + passed[half:]).astype(others.dtype), "seq", 2)
    return own + passed[:half] + last.astype(jnp.float32)


def paired(candidates, gate_values, hist_keys, hist_values, pattern):
    count = CAND_BLOCK
    half = 2 * count
    events = hist_keys.shape[0]
    own, queries, *hists = pack(candidates[0], hist_keys, hist_values)
    kept, sent = hists[:2], hists[2:]
    own = jnp.concatenate([own, swapped(queries, "blk", 1)], axis=0)
    beside = [swapped(x, "blk", 1) for x in sent]
    keys = [jnp.concatenate([x[:events], y[:events]], axis=0) for x, y in zip(kept, beside)]
    values = [jnp.concatenate([x[events:], y[events:]], axis=0) for x, y in zip(kept, beside)]
    hist = jnp.concatenate([keys[0], values[0]], axis=0)
    own = after(own, hist)
    far = swapped(own, "seq", 2)
    far_hist = swapped(hist, "blk", 2)
    near_pack = swapped(jnp.concatenate([own[:, :HEAD_DIM], keys[1]], axis=0), "seq", 1)
    both = swapped(far[:, :HEAD_DIM], "seq", 1)
    near_values = swapped(after(values[1], near_pack), "seq", 1)
    crosses = swapped(jnp.concatenate([own[:, HEAD_DIM:], far[:, HEAD_DIM:]], axis=0), "blk", 2)

    f32, b16 = jnp.float32, jnp.bfloat16
    part = ((half, HEAD_DIM), f32)
    (early,) = call(early_kernel, [((2 * half, HEAD_DIM), f32)], pattern, own, far, keys[0], values[0])
    first, first_far = call(first_kernel, [part, part], pattern, own, far, far_hist, early)
    start, weights, sums = call(
        work_kernel,
        [((4 * half, HEAD_DIM), f32), ((4 * half, 2 * events), b16), ((2 * half, HEAD_DIM), b16)],
        pattern, own, crosses, far, after(keys[1], first), values[1], near_pack, both, keys[0], values[0], far_hist,
        flops=LONG,
    )
    outs = [part, part, ((2 * half, HEAD_DIM), b16)]
    second, second_far, others = call(second_kernel, outs, weights, near_values, start, flops=LONG)
    first, second = (
        reduced(*x) for x in ((first, first_far, sums, "seq", 1), (second, second_far, others, "blk", 2))
    )
    pieces = []
    for x in (first, second):
        pieces += [x[:count], swapped(x[count:], "blk", 1)]
    gate = gate_values[0]
    inputs = [gate, *pieces]
    return call(finish_kernel, [(gate.shape, gate.dtype)], *inputs)[0][None]


def general_kernel(places, pattern, rows, *refs):
    hists, out = refs[:-1], refs[-1]
    blk = lax.axis_index("blk")
    total = None
    for at, hist in enumerate(hists):
        weights = weigh(
            pattern, rows[...], hist[:, :HEAD_DIM], places(blk), hist_places(((0, at),))
        )
        mixed = mix(weights, hist[:, HEAD_DIM:])
        total = mixed if total is None else total + mixed
    out[...] = total


def general_finish_kernel(gate_ref, *refs):
    sums, out_ref = refs[:-1], refs[-1]
    summed = jnp.concatenate([ref[...] for ref in sums], axis=1)
    mean_square = jnp.mean(summed * summed, axis=1, keepdims=True)
    normed = summed * lax.rsqrt(mean_square + 1e-05)
    out_ref[...] = (normed * gate_ref[...].astype(jnp.float32)).astype(out_ref.dtype)


def general(candidates, gate_values, hist_keys, hist_values, pattern):
    hists = []
    for head in range(HEADS):
        wide = slice(head * HEAD_DIM, (head + 1) * HEAD_DIM)
        hists.append(jnp.concatenate([hist_keys[:, wide], hist_values[:, wide]], axis=1))
    gathered = lax.all_gather(candidates[0], "seq", axis=0, tiled=True)
    blocks = gathered.shape[0] // CAND_BLOCK
    masks = range(lax.axis_size("blk"))

    def places(blk):
        return [blk * blocks + i for i in range(blocks)]

    sums = []
    for head in range(HEADS):
        wide = slice(head * HEAD_DIM, (head + 1) * HEAD_DIM)
        around = [swapped(hists[head], "blk", mask) if mask else hists[head] for mask in masks]
        outs = [((gathered.shape[0], HEAD_DIM), jnp.float32)]
        kernel = functools.partial(general_kernel, places)
        (total,) = call(kernel, outs, pattern, gathered[:, wide], *around)
        sums.append(lax.psum_scatter(total, "seq", scatter_dimension=0, tiled=True))
    return pl.pallas_call(
        general_finish_kernel,
        out_shape=jax.ShapeDtypeStruct(gate_values[0].shape, gate_values.dtype),
        in_specs=[VMEM] * (1 + HEADS),
        out_specs=VMEM,
    )(gate_values[0], *sums)[None]


def on_device(candidates, *others):
    if lax.axis_size("seq") == 4 and candidates.shape[1] == CAND_BLOCK:
        return paired(candidates, *others)
    return general(candidates, *others)


def solution(mesh):
    in_specs = (
        P(("groups", "blk"), "seq", None),
        P(("groups", "blk"), "seq", None),
        P(("groups", "seq", "blk"), None),
        P(("groups", "seq", "blk"), None),
        P("groups", None),
    )
    out_specs = P(("groups", "blk"), "seq", None)
    return jax.shard_map(
        on_device, mesh=mesh, in_specs=in_specs, out_specs=out_specs, check_vma=False
    )
```

```python
import functools

import jax
import jax.numpy as jnp
from jax import lax
from jax.experimental import pallas as pl
from jax.experimental.pallas import tpu as pltpu
from jax.sharding import PartitionSpec as P

HEADS = 4
HEAD_DIM = 128
CAND_BLOCK = 128
HALF_SCALE = 0.5 * HEAD_DIM ** (-0.5)
LONG = 10**10
PAIR = 2 * HEAD_DIM
ALONG = ((0, 0), (1, 0), (2, 0), (3, 0))
SQUARE = ((0, 0), (0, 2), (2, 0), (2, 2))
PAIRED = ((0, 0), (0, 1))
ACROSS = ((0, 2), (0, 3))
BESIDE = ((1, 0), (1, 1))
VMEM_LIMIT = 48 * 1024 * 1024
PARAMS = pltpu.CompilerParams(vmem_limit_bytes=VMEM_LIMIT)
COST = pl.CostEstimate(flops=1, transcendentals=0, bytes_accessed=1)
VMEM = pl.BlockSpec(memory_space=pltpu.VMEM)


def swapped(block, axis, mask):
    size = lax.axis_size(axis)
    return lax.ppermute(block, axis, [(i, i ^ mask) for i in range(size)])


def after(block, *others):
    return lax.optimization_barrier((block, *others))[0]


def pack_kernel(queries, keys, values, *refs):
    outs, sems = refs[:-1], refs[-1]
    kept_queries, sent_queries, kept, sent = outs[0], outs[1], outs[2:4], outs[4:]
    core = lax.rem(lax.axis_index("blk"), 2)
    count = keys.shape[0]
    copies = []

    def copy(source, target):
        copies.append(pltpu.make_async_copy(source, target, sems.at[len(copies)]))
        copies[-1].start()

    def columns(side, at, width):
        return pl.ds(pl.multiple_of(side * PAIR + at * HEAD_DIM, HEAD_DIM), width)

    copy(queries.at[:, columns(1 - core, 0, PAIR)], sent_queries)
    copy(queries.at[:, columns(core, 0, PAIR)], kept_queries)
    targets = [part for block in sent for part in (block.at[:count], block.at[count:])]
    for at in range(2):
        copy(keys.at[:, columns(core, at, HEAD_DIM)], kept[at].at[:count])
        copy(values.at[:, columns(core, at, HEAD_DIM)], kept[at].at[count:])
        copy(keys.at[:, columns(1 - core, at, HEAD_DIM)], targets[2 * at])
        copy(values.at[:, columns(1 - core, at, HEAD_DIM)], targets[2 * at + 1])
    for each in copies:
        each.wait()


def pack(queries, keys, values):
    row_shape = jax.ShapeDtypeStruct((queries.shape[0], PAIR), queries.dtype)
    both_shape = jax.ShapeDtypeStruct((2 * keys.shape[0], HEAD_DIM), keys.dtype)
    return pl.pallas_call(
        pack_kernel,
        out_shape=[row_shape] * 2 + [both_shape] * 4,
        in_specs=[pl.BlockSpec(memory_space=pltpu.HBM)] * 3,
        out_specs=[VMEM] * 6,
        scratch_shapes=[pltpu.SemaphoreType.DMA((10,))],
        compiler_params=PARAMS,
        cost_estimate=COST,
    )(*(pltpu.with_memory_space_constraint(x, pltpu.HBM) for x in (queries, keys, values)))


def weigh(pattern_ref, queries, keys, places, columns):
    events = keys.shape[0] // len(columns)
    scores = lax.dot_general(
        queries, keys, (((1,), (1,)), ((), ())), preferred_element_type=jnp.float32
    )
    rows = []
    for i, place in enumerate(places):
        weights = []
        for j, column in enumerate(columns):
            scale = pattern_ref[place, column].astype(jnp.float32) * HALF_SCALE
            half = scores[
                i * CAND_BLOCK : (i + 1) * CAND_BLOCK, j * events : (j + 1) * events
            ] * scale
            weights.append((half + half * jnp.tanh(half)).astype(jnp.bfloat16))
        rows.append(jnp.concatenate(weights, axis=1))
    return jnp.concatenate(rows, axis=0)


def mix(weights, values):
    return jnp.dot(weights, values, preferred_element_type=jnp.float32)


def head_rows(refs, head):
    wide = slice(head * HEAD_DIM, (head + 1) * HEAD_DIM)
    return jnp.concatenate(
        [ref[...] if ref.shape[1] == HEAD_DIM else ref[:, wide] for ref in refs], axis=0
    )


def row_places(places, sides=(0, 1)):
    seq, blk = lax.axis_index("seq"), lax.axis_index("blk")
    size = lax.axis_size("seq")
    return [(blk ^ across ^ side) * size + (seq ^ near) for near, across in places for side in sides]


def hist_places(places):
    seq, blk = lax.axis_index("seq"), lax.axis_index("blk")
    return [(seq ^ near) * lax.axis_size("blk") + (blk ^ across) for near, across in places]


def early_kernel(pattern, own, far, keys, values, out):
    rows = head_rows((own, far), 0)
    weights = weigh(pattern, rows, keys[...], row_places(ALONG[::2]), hist_places(PAIRED))
    out[...] = mix(weights, values[...])


def first_kernel(pattern, own, far, far_hist, start, own_out, far_out):
    half = own.shape[0]
    events = far_hist.shape[0] // 2
    rows = head_rows((own, far), 0)
    weights = weigh(pattern, rows, far_hist[:events], row_places(ALONG[::2]), hist_places(ACROSS))
    total = mix(weights, far_hist[events:]) + start[...]
    own_out[...] = total[:half]
    far_out[...] = total[half:]


def rest_kernel(pattern, near_pack, both, keys, values, far_hist, out):
    half = both.shape[0]
    events = keys.shape[0]
    rows = head_rows((near_pack.at[:half], both), 0)
    weights = weigh(pattern, rows, keys[...], row_places(ALONG[1::2]), hist_places(PAIRED))
    total = mix(weights, values[...])
    weights = weigh(pattern, rows, far_hist[:events], row_places(ALONG[1::2]), hist_places(ACROSS))
    out[...] = (total + mix(weights, far_hist[events:])).astype(out.dtype)


def weights_kernel(pattern, own, crosses, far, keys, values, near_pack, start, out):
    half = own.shape[0]
    rows = head_rows((own, crosses.at[:half], far, crosses.at[half:]), 1)
    weights = weigh(pattern, rows, keys[...], row_places(SQUARE), hist_places(PAIRED))
    start[...] = mix(weights, values[...])
    out[...] = weigh(pattern, rows, near_pack[half:], row_places(SQUARE), hist_places(BESIDE))


def work_kernel(pattern, own, crosses, far, keys, values, near_pack, both, first_keys, first_values, far_hist, start, weights, out):
    weights_kernel(pattern, own, crosses, far, keys, values, near_pack, start, weights)
    rest_kernel(pattern, near_pack, both, first_keys, first_values, far_hist, out)


def second_kernel(weights, near_values, start, own, far, others):
    total = mix(weights[...], near_values[...]) + start[...]
    half = own.shape[0]
    own[...] = total[:half]
    far[...] = total[2 * half : 3 * half]
    others[:half] = total[half : 2 * half].astype(others.dtype)
    others[half:] = total[3 * half :].astype(others.dtype)


def call(kernel, outs, *inputs, flops=1):
    return pl.pallas_call(
        kernel,
        out_shape=[jax.ShapeDtypeStruct(shape, kind) for shape, kind in outs],
        in_specs=[
            pl.BlockSpec(memory_space=pltpu.SMEM) if x.dtype == jnp.int32 else VMEM for x in inputs
        ],
        out_specs=[VMEM] * len(outs),
        compiler_params=PARAMS,
        cost_estimate=pl.CostEstimate(flops=flops, transcendentals=0, bytes_accessed=1),
    )(*inputs)


def finish_kernel(gate_ref, first_mine, first_theirs, second_mine, second_theirs, out_ref):
    core = lax.rem(lax.axis_index("blk"), 2)
    mine = jnp.concatenate([first_mine[...], second_mine[...]], axis=1)
    theirs = jnp.concatenate([first_theirs[...], second_theirs[...]], axis=1).astype(jnp.float32)
    squares = jnp.sum(mine * mine, axis=1, keepdims=True)
    squares = squares + jnp.sum(theirs * theirs, axis=1, keepdims=True)
    factor = lax.rsqrt(squares / (HEADS * HEAD_DIM) + 1e-05)
    first = jnp.where(core == 0, mine, theirs) * factor
    second = jnp.where(core == 0, theirs, mine) * factor
    gate = gate_ref[...].astype(jnp.float32)
    out_ref[:, :PAIR] = (first * gate[:, :PAIR]).astype(out_ref.dtype)
    out_ref[:, PAIR:] = (second * gate[:, PAIR:]).astype(out_ref.dtype)


def reduced(own, far, others, axis, mask):
    half = own.shape[0]
    passed = swapped(others, axis, mask).astype(jnp.float32)
    last = swapped((far + passed[half:]).astype(others.dtype), "seq", 2)
    return own + passed[:half] + last.astype(jnp.float32)


def paired(candidates, gate_values, hist_keys, hist_values, pattern):
    count = CAND_BLOCK
    half = 2 * count
    events = hist_keys.shape[0]
    own, queries, *hists = pack(candidates[0], hist_keys, hist_values)
    kept, sent = hists[:2], hists[2:]
    own = jnp.concatenate([own, swapped(queries, "blk", 1)], axis=0)
    beside = [swapped(x, "blk", 1) for x in sent]
    keys = [jnp.concatenate([x[:events], y[:events]], axis=0) for x, y in zip(kept, beside)]
    values = [jnp.concatenate([x[events:], y[events:]], axis=0) for x, y in zip(kept, beside)]
    hist = jnp.concatenate([keys[0], values[0]], axis=0)
    own = after(own, hist)
    far = swapped(own, "seq", 2)
    far_hist = swapped(hist, "blk", 2)
    near_pack = swapped(jnp.concatenate([own[:, :HEAD_DIM], keys[1]], axis=0), "seq", 1)
    both = swapped(far[:, :HEAD_DIM], "seq", 1)
    near_values = swapped(after(values[1], near_pack), "seq", 1)
    crosses = swapped(jnp.concatenate([own[:, HEAD_DIM:], far[:, HEAD_DIM:]], axis=0), "blk", 2)

    f32, b16 = jnp.float32, jnp.bfloat16
    part = ((half, HEAD_DIM), f32)
    (early,) = call(early_kernel, [((2 * half, HEAD_DIM), f32)], pattern, own, far, keys[0], values[0])
    first, first_far = call(first_kernel, [part, part], pattern, own, far, far_hist, early)
    start, weights, sums = call(
        work_kernel,
        [((4 * half, HEAD_DIM), f32), ((4 * half, 2 * events), b16), ((2 * half, HEAD_DIM), b16)],
        pattern, own, crosses, far, after(keys[1], first), values[1], near_pack, both, keys[0], values[0], far_hist,
        flops=LONG,
    )
    outs = [part, part, ((2 * half, HEAD_DIM), b16)]
    second, second_far, others = call(second_kernel, outs, weights, near_values, start, flops=LONG)
    first, second = (
        reduced(*x) for x in ((first, first_far, sums, "seq", 1), (second, second_far, others, "blk", 2))
    )
    pieces = []
    for x in (first, second):
        pieces += [x[:count], swapped(x[count:].astype(b16), "blk", 1)]
    gate = gate_values[0]
    inputs = [gate, *pieces]
    return call(finish_kernel, [(gate.shape, gate.dtype)], *inputs)[0][None]


def general_kernel(places, pattern, rows, *refs):
    hists, out = refs[:-1], refs[-1]
    blk = lax.axis_index("blk")
    total = None
    for at, hist in enumerate(hists):
        weights = weigh(
            pattern, rows[...], hist[:, :HEAD_DIM], places(blk), hist_places(((0, at),))
        )
        mixed = mix(weights, hist[:, HEAD_DIM:])
        total = mixed if total is None else total + mixed
    out[...] = total


def general_finish_kernel(gate_ref, *refs):
    sums, out_ref = refs[:-1], refs[-1]
    summed = jnp.concatenate([ref[...] for ref in sums], axis=1)
    mean_square = jnp.mean(summed * summed, axis=1, keepdims=True)
    normed = summed * lax.rsqrt(mean_square + 1e-05)
    out_ref[...] = (normed * gate_ref[...].astype(jnp.float32)).astype(out_ref.dtype)


def general(candidates, gate_values, hist_keys, hist_values, pattern):
    hists = []
    for head in range(HEADS):
        wide = slice(head * HEAD_DIM, (head + 1) * HEAD_DIM)
        hists.append(jnp.concatenate([hist_keys[:, wide], hist_values[:, wide]], axis=1))
    gathered = lax.all_gather(candidates[0], "seq", axis=0, tiled=True)
    blocks = gathered.shape[0] // CAND_BLOCK
    masks = range(lax.axis_size("blk"))

    def places(blk):
        return [blk * blocks + i for i in range(blocks)]

    sums = []
    for head in range(HEADS):
        wide = slice(head * HEAD_DIM, (head + 1) * HEAD_DIM)
        around = [swapped(hists[head], "blk", mask) if mask else hists[head] for mask in masks]
        outs = [((gathered.shape[0], HEAD_DIM), jnp.float32)]
        kernel = functools.partial(general_kernel, places)
        (total,) = call(kernel, outs, pattern, gathered[:, wide], *around)
        sums.append(lax.psum_scatter(total, "seq", scatter_dimension=0, tiled=True))
    return pl.pallas_call(
        general_finish_kernel,
        out_shape=jax.ShapeDtypeStruct(gate_values[0].shape, gate_values.dtype),
        in_specs=[VMEM] * (1 + HEADS),
        out_specs=VMEM,
    )(gate_values[0], *sums)[None]


def on_device(candidates, *others):
    if lax.axis_size("seq") == 4 and candidates.shape[1] == CAND_BLOCK:
        return paired(candidates, *others)
    return general(candidates, *others)


def solution(mesh):
    in_specs = (
        P(("groups", "blk"), "seq", None),
        P(("groups", "blk"), "seq", None),
        P(("groups", "seq", "blk"), None),
        P(("groups", "seq", "blk"), None),
        P("groups", None),
    )
    out_specs = P(("groups", "blk"), "seq", None)
    return jax.shard_map(
        on_device, mesh=mesh, in_specs=in_specs, out_specs=out_specs, check_vma=False
    )
```
